32 devices in a mesh: rep: 2 (over x), dp: 16 (over z, y, core).
Axes of the slice: x: 2, y: 2, z: 4, core: 2. Of those that a mesh axis runs over, the one named last changes fastest.
Arguments:
- queries: bfloat16 [12288, 6144], P(('rep', 'dp')), parts along dimension 0, may hold values from -48 to 48
- latents: bfloat16 [12288, 576], P(('rep', 'dp')), parts along dimension 0, may hold values from -48 to 48
- kv_weight: bfloat16 [512, 6144], replicated, may hold values from -1 to 1
- lengths: int32 [192], P('rep'), parts along dimension 0, may hold values from 1 to 128, 6144 in all
Outputs:
- attn_out: bfloat16 [12288, 2048], P(('rep', 'dp')), parts along dimension 0
- hessian: float32 [4096, 2048], P(('rep', 'dp')), parts along dimension 0
The draws below stay inside these ranges and needn't reach their ends.
There are 2 independent parts, one for each index of `rep`. The reference program is written for one: setup_inputs(seed, part) draws one part's arguments, and reference() takes and returns one part's arrays. A program takes and returns all parts, laid end to end along the dimension named above; an argument that names none is the same for every part. Nothing has to cross between parts.
Inputs may be any that keep to these rules, and one draw needn't show every extreme that they name: lengths of the 96 traces packed end to end in order; they sum to 6144 and the largest is exactly 128.
All inputs are finite; a program needn't handle non-finite values.
Results may differ from the reference program's by a relative error of at most 0.0065.
Values may be sent and summed in bfloat16 or wider, within the bound.
A program may use at most 128 MiB of HBM per device.

```python
import math
import jax
import jax.numpy as jnp
import numpy as np
from jax import lax

HEADS = 32
NOPE = 128
ROPE = 64
V_DIM = 64
KV_RANK = 512
MAXLEN = 128
TOK_DEV = 384
TOKENS = 6144
TRACES = 96
OUT_WIDTH = 2048


def shared_rope(key):
    base_rope = jnp.clip(jax.random.normal(key, (TOKENS, ROPE), jnp.float32), -4.0, 4.0)
    return base_rope


def draw_latents(key, part):
    base_rope = shared_rope(key)
    key = jax.random.fold_in(key, 11)
    content_key = jax.random.fold_in(key, 0)
    content = jnp.clip(jax.random.normal(content_key, (TOKENS, KV_RANK), jnp.float32), -4.0, 4.0)
    rope_part = base_rope
    return jnp.concatenate([content, rope_part], axis=1).astype(jnp.bfloat16)


def draw_queries(key, part):
    key = jax.random.fold_in(key, 12)
    content_key = jax.random.fold_in(key, 0)
    entries = jnp.clip(jax.random.normal(content_key, (TOKENS, HEADS, NOPE + ROPE), jnp.float32), -4.0, 4.0)
    return entries.reshape(TOKENS, HEADS * (NOPE + ROPE)).astype(jnp.bfloat16)


def draw_kv_weight(key, part):
    key = jax.random.fold_in(key, 13)
    private_key, common_key, scale_key = jax.random.split(key, 3)
    private = jnp.clip(jax.random.normal(private_key, (KV_RANK, HEADS, NOPE + V_DIM), jnp.float32), -4.0, 4.0)
    common = jnp.clip(jax.random.normal(common_key, (KV_RANK, 1, V_DIM), jnp.float32), -4.0, 4.0)
    column_scale = jnp.exp(jax.random.uniform(scale_key, (1, HEADS, V_DIM), jnp.float32, math.log(0.5), math.log(4.0)))
    value_part = column_scale * (private[:, :, NOPE:] + 0.6 * common) / math.sqrt(1.36 * KV_RANK)
    keys_part = private[:, :, :NOPE] / math.sqrt(KV_RANK)
    joined = jnp.concatenate([keys_part, value_part], axis=2)
    return jnp.clip(joined, -1.0, 1.0).reshape(KV_RANK, HEADS * (NOPE + V_DIM)).astype(jnp.bfloat16)


def split_up(number_of, total, limit, slope):
    portions = [(1 << 20) // math.isqrt(grade ** slope) + 1 for grade in range(2, number_of + 1)]
    surplus, given = total - limit - (number_of - 1), [1] * (number_of - 1)
    while surplus > 0:
        candidates = [i for i in range(number_of - 1) if given[i] < limit]
        mass, remaining = sum([portions[i] for i in candidates]), surplus
        for i in candidates:
            extra = min(limit - given[i], max(1, remaining * portions[i] // mass), surplus)
            given[i] = given[i] + extra
            surplus = surplus - extra
    return np.array([limit] + given)


def ragged(key, amount, total, most, lean):
    if amount == 2:
        one = jax.random.randint(key, (), max(1, total - most), min(most, total - 1) + 1)
        return jnp.stack([one, total - one])
    tallies = jnp.asarray(split_up(amount, total, most, lean), jnp.int32)
    couples = (amount - 1) // 2
    giver, receiver = tallies[1:1 + 2 * couples:2], tallies[2:2 + 2 * couples:2]
    margin = jnp.minimum(giver - 1, most - receiver)
    moved = jax.random.randint(jax.random.fold_in(key, 1), (couples,), 0, 1 << 20) % (margin + 1)
    tallies = tallies.at[1:1 + 2 * couples:2].set(giver - moved).at[2:2 + 2 * couples:2].set(receiver + moved)
    return tallies[jax.random.permutation(jax.random.fold_in(key, 2), amount)]


def setup_inputs(seed: int = 0, part: int = 0) -> dict:
    seeds = jax.random.split(jax.random.key(seed), 5)
    part_splits = jax.random.split(jax.random.fold_in(seeds[4], part), 5)
    return {
        "queries": draw_queries(jax.random.fold_in(jax.random.fold_in(seeds[4], part), 71), part),
        "latents": draw_latents(jax.random.fold_in(jax.random.fold_in(seeds[4], part), 71), part),
        "kv_weight": draw_kv_weight(jax.random.fold_in(seeds[4], 71), part),
        "lengths": ragged(part_splits[3], TRACES, TOKENS, MAXLEN, 1).astype(jnp.int32),
    }


MASKED = -1e+30

def reference(queries, latents, kv_weight, lengths):
    score_scale = 1.0 / math.sqrt(NOPE + ROPE)
    trace_ends = jnp.cumsum(lengths).astype(jnp.int32)
    kv_up = jnp.dot(latents[:, :KV_RANK], kv_weight, preferred_element_type=jnp.float32).astype(jnp.bfloat16)
    kv_up = lax.optimization_barrier(kv_up).reshape(TOKENS, HEADS, NOPE + V_DIM)
    padded_kv = jnp.concatenate([jnp.zeros((MAXLEN, HEADS, NOPE + V_DIM), jnp.bfloat16), kv_up], axis=0)
    padded_rope = jnp.concatenate([jnp.zeros((MAXLEN, ROPE), jnp.bfloat16), latents[:, KV_RANK:]], axis=0)
    query_heads = queries.reshape(TOKENS, HEADS, NOPE + ROPE)

    def one_block(block_index):
        first_row = block_index * TOK_DEV
        query_block = lax.dynamic_slice_in_dim(query_heads, first_row, TOK_DEV, 0).astype(jnp.float32)
        key_block = lax.dynamic_slice_in_dim(padded_kv, first_row, TOK_DEV + MAXLEN, 0).astype(jnp.float32)
        rope_block = lax.dynamic_slice_in_dim(padded_rope, first_row, TOK_DEV + MAXLEN, 0).astype(jnp.float32)
        query_pos = first_row + jnp.arange(TOK_DEV, dtype=jnp.int32)
        key_pos = first_row - MAXLEN + jnp.arange(TOK_DEV + MAXLEN, dtype=jnp.int32)
        query_trace = jnp.searchsorted(trace_ends, query_pos, side='right')
        key_trace = jnp.searchsorted(trace_ends, key_pos, side='right')
        allowed = (query_trace[:, None] == key_trace[None, :]) & (key_pos[None, :] <= query_pos[:, None]) & (key_pos[None, :] >= 0)
        scores = jnp.einsum('qhd,khd->hqk', query_block[:, :, :NOPE], key_block[:, :, :NOPE])
        scores = scores + jnp.einsum('qhd,kd->hqk', query_block[:, :, NOPE:], rope_block)
        scores = jnp.where(allowed[None], scores * score_scale, MASKED)
        row_max = lax.optimization_barrier(jnp.max(scores, axis=-1, keepdims=True))
        weights = jnp.exp(scores - row_max)
        weights = (weights / lax.optimization_barrier(jnp.sum(weights, axis=-1, keepdims=True))).astype(jnp.bfloat16)
        weights = lax.optimization_barrier(weights).astype(jnp.float32)
        mixed_values = jnp.einsum('hqk,khd->qhd', weights, key_block[:, :, NOPE:])
        return mixed_values.reshape(TOK_DEV, OUT_WIDTH).astype(jnp.bfloat16)
    blocks = lax.map(one_block, jnp.arange(TOKENS // TOK_DEV, dtype=jnp.int32))
    attn_out = blocks.reshape(TOKENS, OUT_WIDTH)
    hessian = lax.dot_general(attn_out, attn_out, (((0,), (0,)), ((), ())), preferred_element_type=jnp.float32) / TOKENS
    return (attn_out, hessian)
```

```python
import math

import jax
import jax.numpy as jnp
from jax import lax
from jax.experimental import pallas as pl
from jax.experimental.pallas import tpu as pltpu
from jax.sharding import PartitionSpec as P

HEADS = 32
NOPE = 128
ROPE = 64
V_DIM = 64
KV_RANK = 512
MAXLEN = 128
OUT_WIDTH = 2048

MASKED = -1e30
BLOCK = 128
HEAD_WIDTH = NOPE + ROPE
PAIR = 2 * HEAD_WIDTH
PAIRS_PER_STEP = 2
STRIP = 9 * BLOCK
MESH = pl.DeviceIdType.MESH
EXP_SCALE = math.log2(math.e) / math.sqrt(NOPE + ROPE)


def attention_kernel(window_ref, start_ref, weight_ref, query_ref, out_ref, bias_ref):
    rows = query_ref.shape[0]
    blocks = rows // BLOCK

    @pl.when(pl.program_id(0) == 0)
    def _():
        for b in range(blocks):
            start = start_ref[b * BLOCK : (b + 1) * BLOCK, :]
            key = lax.broadcasted_iota(jnp.int32, (BLOCK, 2 * BLOCK), 1) + (b - 1) * BLOCK
            query = lax.broadcasted_iota(jnp.int32, (BLOCK, 2 * BLOCK), 0) + b * BLOCK
            allowed = (key <= query) & (key >= start)
            bias_ref[b * BLOCK : (b + 1) * BLOCK, :] = jnp.where(allowed, 0.0, MASKED)

    content = window_ref[:, :KV_RANK]
    rope_low = window_ref[:, KV_RANK : KV_RANK + 128]
    rope_high = window_ref[:, KV_RANK + 128 :]
    keys_rows = window_ref.shape[0]
    low = lax.broadcasted_iota(jnp.int32, (keys_rows, 128), 1) < 64
    low_out = lax.broadcasted_iota(jnp.int32, (BLOCK, 128), 1) < 64
    one = jnp.ones((keys_rows, 128), jnp.bfloat16)
    zero = jnp.zeros((keys_rows, 128), jnp.bfloat16)
    for pair in range(PAIRS_PER_STEP):
        at = pair * PAIR
        kv = jnp.dot(
            content, weight_ref[:, at : at + PAIR], preferred_element_type=jnp.float32
        ).astype(jnp.bfloat16)
        first, second, third = kv[:, :128], kv[:, 128:256], kv[:, 256:384]
        keys = (
            jnp.concatenate([first, rope_low], axis=1),
            jnp.concatenate(
                [jnp.where(low, zero, second), jnp.where(low, third, rope_high)], axis=1
            ),
        )
        values = (jnp.where(low, second, one), jnp.where(low, one, third))
        for b in range(blocks):
            rows_at = slice(b * BLOCK, (b + 1) * BLOCK)
            keys_at = slice(b * BLOCK, (b + 2) * BLOCK)
            bias = bias_ref[rows_at, :]
            mixed = []
            for head in range(2):
                query = query_ref[rows_at, at + head * 128 : at + head * 128 + 256]
                scores = lax.dot_general(
                    query,
                    keys[head][keys_at],
                    (((1,), (1,)), ((), ())),
                    preferred_element_type=jnp.float32,
                )
                scores = scores + bias
                top = jnp.max(scores, axis=1, keepdims=True)
                weights = jnp.exp2((scores - top) * EXP_SCALE).astype(jnp.bfloat16)
                mixed.append(
                    jnp.dot(weights, values[head][keys_at], preferred_element_type=jnp.float32)
                )
            total = pltpu.roll(jnp.where(low_out, mixed[1], mixed[0]), 64, 1)
            result = jnp.where(low_out, mixed[0], mixed[1]) / total
            out_ref[rows_at, pair * 128 : (pair + 1) * 128] = result.astype(jnp.bfloat16)


def attention(window, start, kv_weight, queries):
    rows = queries.shape[0]
    span = PAIR * PAIRS_PER_STEP
    return pl.pallas_call(
        attention_kernel,
        grid=(queries.shape[1] // span,),
        in_specs=[
            pl.BlockSpec(window.shape, lambda i: (0, 0)),
            pl.BlockSpec(start.shape, lambda i: (0, 0)),
            pl.BlockSpec((KV_RANK, span), lambda i: (0, i)),
            pl.BlockSpec((rows, span), lambda i: (0, i)),
        ],
        out_specs=pl.BlockSpec((rows, PAIRS_PER_STEP * 128), lambda i: (0, i)),
        out_shape=jax.ShapeDtypeStruct((rows, OUT_WIDTH), jnp.bfloat16),
        scratch_shapes=[pltpu.VMEM((rows, 2 * BLOCK), jnp.float32)],
        compiler_params=pltpu.CompilerParams(vmem_limit_bytes=40 * 1024 * 1024),
    )(window, start, kv_weight, queries)


def hessian_kernel(
    devices,
    inverse_count,
    a_ref,
    out_ref,
    a_all,
    y_send,
    y_recv,
    z_send,
    z_recv,
    t_send,
    t_recv,
    local_sem,
    pair_send_sem,
    pair_recv_sem,
    y_send_sem,
    y_recv_sem,
    z_send_sem,
    z_recv_sem,
    t_send_sem,
    t_recv_sem,
):
    rows = a_ref.shape[0]
    extra = STRIP - BLOCK
    zs = devices // 4
    me = lax.axis_index("dp")
    rep = lax.axis_index("rep")
    core = lax.rem(me, 2)
    y = lax.rem(me // 2, 2)
    z = me // 4

    def index_of(z_at, y_at):
        return (z_at * 2 + y_at) * 2 + core

    def other(k):
        return lax.rem(me + k, devices)

    partner = z * 4 + y * 2 + (1 - core)

    barrier = pltpu.get_barrier_semaphore()
    for k in range(1, devices):
        pl.semaphore_signal(barrier, inc=1, device_id=(rep, other(k)), device_id_type=MESH)
    own = [
        pltpu.make_async_copy(a_ref, a_all.at[0:rows, 0:OUT_WIDTH], local_sem.at[0]),
        pltpu.make_async_copy(
            a_ref.at[:, 0:extra],
            a_all.at[0:rows, OUT_WIDTH : OUT_WIDTH + extra],
            local_sem.at[1],
        ),
    ]
    for copy in own:
        copy.start()
    pl.semaphore_wait(barrier, devices - 1)

    pair_copies = [
        pltpu.make_async_remote_copy(
            src_ref=a_ref,
            dst_ref=a_all.at[rows : 2 * rows, 0:OUT_WIDTH],
            send_sem=pair_send_sem.at[0],
            recv_sem=pair_recv_sem.at[0],
            device_id=(rep, partner),
            device_id_type=MESH,
        ),
        pltpu.make_async_remote_copy(
            src_ref=a_ref.at[:, 0:extra],
            dst_ref=a_all.at[rows : 2 * rows, OUT_WIDTH : OUT_WIDTH + extra],
            send_sem=pair_send_sem.at[1],
            recv_sem=pair_recv_sem.at[1],
            device_id=(rep, partner),
            device_id_type=MESH,
        ),
    ]
    for copy in pair_copies:
        copy.start()
    for copy in own:
        copy.wait()
    for copy in pair_copies:
        copy.wait()

    def strip(owner):
        at = pl.multiple_of(owner * BLOCK, BLOCK)
        return lax.dot_general(
            a_all[:, pl.ds(at, BLOCK)],
            a_all[:, pl.ds(at, STRIP)],
            (((0,), (0,)), ((), ())),
            preferred_element_type=jnp.float32,
        )

    y_copies = []
    for j in range(zs):
        z_at = lax.rem(z + 1 + j, zs)
        y_send[j] = strip(index_of(z_at, 1 - y)).astype(jnp.bfloat16)
        copy = pltpu.make_async_remote_copy(
            src_ref=y_send.at[j],
            dst_ref=y_recv.at[j],
            send_sem=y_send_sem.at[j],
            recv_sem=y_recv_sem.at[j],
            device_id=(rep, index_of(z, 1 - y)),
            device_id_type=MESH,
        )
        copy.start()
        y_copies.append(copy)

    z_copies = []
    for j in range(zs):
        z_at = lax.rem(z + 1 + j, zs)
        mine = strip(index_of(z_at, y))
        y_copies[j].wait_recv()
        mine = mine + y_recv[j].astype(jnp.float32)
        if j < zs - 1:
            z_send[j] = mine.astype(jnp.bfloat16)
            copy = pltpu.make_async_remote_copy(
                src_ref=z_send.at[j],
                dst_ref=z_recv.at[j],
                send_sem=z_send_sem.at[j],
                recv_sem=z_recv_sem.at[j],
                device_id=(rep, index_of(z_at, y)),
                device_id_type=MESH,
            )
            copy.start()
            z_copies.append(copy)
        else:
            total = mine
    for j in range(zs - 1):
        z_copies[j].wait_recv()
        total = total + z_recv[j].astype(jnp.float32)
    total = total * inverse_count

    t_copies = []
    for k in range(1, 8):
        t_send[k - 1] = total[:, k * BLOCK : (k + 1) * BLOCK].T.astype(jnp.bfloat16)
        copy = pltpu.make_async_remote_copy(
            src_ref=t_send.at[k - 1],
            dst_ref=t_recv.at[k - 1],
            send_sem=t_send_sem.at[k - 1],
            recv_sem=t_recv_sem.at[k - 1],
            device_id=(rep, other(k)),
            device_id_type=MESH,
        )
        copy.start()
        t_copies.append(copy)
    for k in range(9):
        at = pl.multiple_of(other(k) * BLOCK, BLOCK)
        out_ref[:, pl.ds(at, BLOCK)] = total[:, k * BLOCK : (k + 1) * BLOCK]
    for k in range(1, 8):
        t_copies[k - 1].wait_recv()
        at = pl.multiple_of(other(devices - k) * BLOCK, BLOCK)
        out_ref[:, pl.ds(at, BLOCK)] = t_recv[k - 1].astype(jnp.float32)
    for copy in y_copies + z_copies + t_copies:
        copy.wait_send()


def fused_hessian(attn_out, devices, inverse_count):
    rows = attn_out.shape[0]
    zs = devices // 4
    vmem = pl.BlockSpec(memory_space=pltpu.VMEM)

    def body(*refs):
        hessian_kernel(devices, inverse_count, *refs)

    return pl.pallas_call(
        body,
        out_shape=jax.ShapeDtypeStruct((BLOCK, OUT_WIDTH), jnp.float32),
        in_specs=[vmem],
        out_specs=vmem,
        scratch_shapes=[
            pltpu.VMEM((2 * rows, OUT_WIDTH + STRIP - BLOCK), jnp.bfloat16),
            pltpu.VMEM((zs, BLOCK, STRIP), jnp.bfloat16),
            pltpu.VMEM((zs, BLOCK, STRIP), jnp.bfloat16),
            pltpu.VMEM((zs - 1, BLOCK, STRIP), jnp.bfloat16),
            pltpu.VMEM((zs - 1, BLOCK, STRIP), jnp.bfloat16),
            pltpu.VMEM((7, BLOCK, BLOCK), jnp.bfloat16),
            pltpu.VMEM((7, BLOCK, BLOCK), jnp.bfloat16),
            pltpu.SemaphoreType.DMA((2,)),
            pltpu.SemaphoreType.DMA((2,)),
            pltpu.SemaphoreType.DMA((2,)),
            pltpu.SemaphoreType.DMA((zs,)),
            pltpu.SemaphoreType.DMA((zs,)),
            pltpu.SemaphoreType.DMA((zs - 1,)),
            pltpu.SemaphoreType.DMA((zs - 1,)),
            pltpu.SemaphoreType.DMA((7,)),
            pltpu.SemaphoreType.DMA((7,)),
        ],
        compiler_params=pltpu.CompilerParams(
            collective_id=0, has_side_effects=True, vmem_limit_bytes=40 * 1024 * 1024
        ),
    )(attn_out)


def per_device(queries, latents, kv_weight, lengths):
    devices = lax.axis_size("dp")
    device = lax.axis_index("dp")
    rows = queries.shape[0]
    inverse_count = 1.0 / (rows * devices)
    halo = lax.ppermute(
        latents[rows - MAXLEN :], "dp", [(source, source + 1) for source in range(devices - 1)]
    )
    window = jnp.concatenate([halo, latents], axis=0)
    rope = window[:, KV_RANK:]
    blank = jnp.zeros((rows + MAXLEN, 2 * (128 - ROPE)), window.dtype)
    window = jnp.concatenate([window, blank, rope], axis=1)

    traces = lengths.shape[0]
    order = jnp.arange(traces, dtype=jnp.int32)
    ends = jnp.sum(jnp.where(order[None, :] <= order[:, None], lengths[None, :], 0), axis=1)
    first_row = device * rows
    position = first_row + jnp.arange(rows, dtype=jnp.int32)
    start = jnp.max(jnp.where(ends[None, :] <= position[:, None], ends[None, :], 0), axis=1)
    start = (start - first_row)[:, None]

    attn_out = attention(window, start, kv_weight, queries)
    if devices * BLOCK == OUT_WIDTH:
        return attn_out, fused_hessian(attn_out, devices, inverse_count)
    partial = lax.dot_general(
        attn_out, attn_out, (((0,), (0,)), ((), ())), preferred_element_type=jnp.float32
    )
    hessian = lax.psum_scatter(partial, "dp", scatter_dimension=0, tiled=True)
    return attn_out, hessian * inverse_count


def solution(mesh):
    placed = (P(("rep", "dp"), None), P(("rep", "dp"), None), P(), P("rep"))
    return jax.shard_map(
        per_device,
        mesh=mesh,
        in_specs=placed,
        out_specs=(P(("rep", "dp"), None), P(("rep", "dp"), None)),
        check_vma=False,
    )
```

```python
import math

import jax
import jax.numpy as jnp
from jax import lax
from jax.experimental import pallas as pl
from jax.experimental.pallas import tpu as pltpu
from jax.sharding import PartitionSpec as P

HEADS = 32
NOPE = 128
ROPE = 64
V_DIM = 64
KV_RANK = 512
MAXLEN = 128
OUT_WIDTH = 2048

MASKED = -1e30
BLOCK = 128
HEAD_WIDTH = NOPE + ROPE
PAIR = 2 * HEAD_WIDTH
PAIRS_PER_STEP = 2
STRIP = 9 * BLOCK
LAG = 2
MESH = pl.DeviceIdType.MESH
EXP_SCALE = math.log2(math.e) / math.sqrt(NOPE + ROPE)


def attention_kernel(window_ref, start_ref, weight_ref, query_ref, out_ref, bias_ref):
    rows = query_ref.shape[0]
    blocks = rows // BLOCK

    @pl.when(pl.program_id(0) == 0)
    def _():
        for b in range(blocks):
            start = start_ref[b * BLOCK : (b + 1) * BLOCK, :]
            key = lax.broadcasted_iota(jnp.int32, (BLOCK, 2 * BLOCK), 1) + (b - 1) * BLOCK
            query = lax.broadcasted_iota(jnp.int32, (BLOCK, 2 * BLOCK), 0) + b * BLOCK
            allowed = (key <= query) & (key >= start)
            bias_ref[b * BLOCK : (b + 1) * BLOCK, :] = jnp.where(allowed, 0.0, MASKED)

    content = window_ref[:, :KV_RANK]
    rope_low = window_ref[:, KV_RANK : KV_RANK + 128]
    rope_high = window_ref[:, KV_RANK + 128 :]
    keys_rows = window_ref.shape[0]
    low = lax.broadcasted_iota(jnp.int32, (keys_rows, 128), 1) < 64
    low_out = lax.broadcasted_iota(jnp.int32, (BLOCK, 128), 1) < 64
    one = jnp.ones((keys_rows, 128), jnp.bfloat16)
    zero = jnp.zeros((keys_rows, 128), jnp.bfloat16)
    for pair in range(PAIRS_PER_STEP):
        at = pair * PAIR
        kv = jnp.dot(
            content, weight_ref[:, at : at + PAIR], preferred_element_type=jnp.float32
        ).astype(jnp.bfloat16)
        first, second, third = kv[:, :128], kv[:, 128:256], kv[:, 256:384]
        keys = (
            jnp.concatenate([first, rope_low], axis=1),
            jnp.concatenate(
                [jnp.where(low, zero, second), jnp.where(low, third, rope_high)], axis=1
            ),
        )
        values = (jnp.where(low, second, one), jnp.where(low, one, third))
        for b in range(blocks):
            rows_at = slice(b * BLOCK, (b + 1) * BLOCK)
            keys_at = slice(b * BLOCK, (b + 2) * BLOCK)
            bias = bias_ref[rows_at, :]
            mixed = []
            for head in range(2):
                query = query_ref[rows_at, at + head * 128 : at + head * 128 + 256]
                scores = lax.dot_general(
                    query,
                    keys[head][keys_at],
                    (((1,), (1,)), ((), ())),
                    preferred_element_type=jnp.float32,
                )
                scores = scores + bias
                top = jnp.max(scores, axis=1, keepdims=True)
                weights = jnp.exp2((scores - top) * EXP_SCALE).astype(jnp.bfloat16)
                mixed.append(
                    jnp.dot(weights, values[head][keys_at], preferred_element_type=jnp.float32)
                )
            total = pltpu.roll(jnp.where(low_out, mixed[1], mixed[0]), 64, 1)
            result = jnp.where(low_out, mixed[0], mixed[1]) / total
            out_ref[rows_at, pair * 128 : (pair + 1) * 128] = result.astype(jnp.bfloat16)


def attention(window, start, kv_weight, queries):
    rows = queries.shape[0]
    span = PAIR * PAIRS_PER_STEP
    return pl.pallas_call(
        attention_kernel,
        grid=(queries.shape[1] // span,),
        in_specs=[
            pl.BlockSpec(window.shape, lambda i: (0, 0)),
            pl.BlockSpec(start.shape, lambda i: (0, 0)),
            pl.BlockSpec((KV_RANK, span), lambda i: (0, i)),
            pl.BlockSpec((rows, span), lambda i: (0, i)),
        ],
        out_specs=pl.BlockSpec((rows, PAIRS_PER_STEP * 128), lambda i: (0, i)),
        out_shape=jax.ShapeDtypeStruct((rows, OUT_WIDTH), jnp.bfloat16),
        scratch_shapes=[pltpu.VMEM((rows, 2 * BLOCK), jnp.float32)],
        compiler_params=pltpu.CompilerParams(vmem_limit_bytes=40 * 1024 * 1024),
    )(window, start, kv_weight, queries)


def fused_kernel(
    devices,
    inverse_count,
    window_ref,
    start_ref,
    weight_ref,
    query_ref,
    out_ref,
    hessian_ref,
    bias_ref,
    a_all,
    z_send,
    z_recv,
    t_send,
    t_recv,
    pair_send_sem,
    pair_recv_sem,
    y_send_sem,
    y_recv_sem,
    pass_send_sem,
    pass_recv_sem,
    z_send_sem,
    z_recv_sem,
    t_send_sem,
    t_recv_sem,
):
    rows = query_ref.shape[0]
    width = out_ref.shape[1]
    steps = OUT_WIDTH // width
    zs = devices // 4
    step = pl.program_id(0)
    me = lax.axis_index("dp")
    rep = lax.axis_index("rep")
    core = lax.rem(me, 2)
    y = lax.rem(me // 2, 2)
    z = me // 4

    def index_of(z_at, y_at, core_at):
        return (z_at * 2 + y_at) * 2 + core_at

    def other(k):
        return lax.rem(me + k, devices)

    partner = index_of(z, y, 1 - core)
    across = index_of(z, 1 - y, core)

    def piece_copy(source, target, piece, send_sem, recv_sem, device):
        at = pl.ds(pl.multiple_of(piece * width, width), width)
        return pltpu.make_async_remote_copy(
            src_ref=a_all.at[source * rows : (source + 1) * rows, at],
            dst_ref=a_all.at[target * rows : (target + 1) * rows, at],
            send_sem=send_sem.at[piece],
            recv_sem=recv_sem.at[piece],
            device_id=(rep, device),
            device_id_type=MESH,
        )

    def pair_copy(piece):
        return piece_copy(0, 1, piece, pair_send_sem, pair_recv_sem, partner)

    def y_copy(piece):
        return piece_copy(0, 2, piece, y_send_sem, y_recv_sem, across)

    def pass_copy(piece):
        return piece_copy(2, 3, piece, pass_send_sem, pass_recv_sem, partner)

    @pl.when(step == 0)
    def _():
        barrier = pltpu.get_barrier_semaphore()
        for k in range(1, devices):
            pl.semaphore_signal(barrier, inc=1, device_id=(rep, other(k)), device_id_type=MESH)

    attention_kernel(window_ref, start_ref, weight_ref, query_ref, out_ref, bias_ref)
    a_all[0:rows, pl.ds(pl.multiple_of(step * width, width), width)] = out_ref[...]

    @pl.when(step == 0)
    def _():
        pl.semaphore_wait(pltpu.get_barrier_semaphore(), devices - 1)

    y_copy(step).start()
    pair_copy(step).start()

    @pl.when(step >= LAG)
    def _():
        y_copy(step - LAG).wait_recv()
        pass_copy(step - LAG).start()

    @pl.when(step == steps - 1)
    def _():
        for piece in range(steps - LAG, steps):
            y_copy(piece).wait_recv()
            pass_copy(piece).start()
        for piece in range(steps):
            pair_copy(piece).wait_recv()
            pass_copy(piece).wait_recv()
        a_all[:, OUT_WIDTH:] = a_all[:, : STRIP - BLOCK]

        def strip(owner):
            at = pl.multiple_of(owner * BLOCK, BLOCK)
            return lax.dot_general(
                a_all[:, pl.ds(at, BLOCK)],
                a_all[:, pl.ds(at, STRIP)],
                (((0,), (0,)), ((), ())),
                preferred_element_type=jnp.float32,
            )

        z_copies = []
        for j in range(zs - 1):
            target = index_of(lax.rem(z + 1 + j, zs), y, core)
            z_send[j] = strip(target).astype(jnp.bfloat16)
            copy = pltpu.make_async_remote_copy(
                src_ref=z_send.at[j],
                dst_ref=z_recv.at[j],
                send_sem=z_send_sem.at[j],
                recv_sem=z_recv_sem.at[j],
                device_id=(rep, target),
                device_id_type=MESH,
            )
            copy.start()
            z_copies.append(copy)
        total = strip(me)
        for j in range(zs - 1):
            z_copies[j].wait_recv()
            total = total + z_recv[j].astype(jnp.float32)
        total = total * inverse_count

        t_copies = []
        for k in range(1, 8):
            t_send[k - 1] = total[:, k * BLOCK : (k + 1) * BLOCK].T.astype(jnp.bfloat16)
            copy = pltpu.make_async_remote_copy(
                src_ref=t_send.at[k - 1],
                dst_ref=t_recv.at[k - 1],
                send_sem=t_send_sem.at[k - 1],
                recv_sem=t_recv_sem.at[k - 1],
                device_id=(rep, other(k)),
                device_id_type=MESH,
            )
            copy.start()
            t_copies.append(copy)
        for k in range(9):
            at = pl.multiple_of(other(k) * BLOCK, BLOCK)
            hessian_ref[:, pl.ds(at, BLOCK)] = total[:, k * BLOCK : (k + 1) * BLOCK]
        for k in range(1, 8):
            t_copies[k - 1].wait_recv()
            at = pl.multiple_of(other(devices - k) * BLOCK, BLOCK)
            hessian_ref[:, pl.ds(at, BLOCK)] = t_recv[k - 1].astype(jnp.float32)
        for piece in range(steps):
            pair_copy(piece).wait_send()
            y_copy(piece).wait_send()
            pass_copy(piece).wait_send()
        for copy in z_copies + t_copies:
            copy.wait_send()


def fused(window, start, kv_weight, queries, devices, inverse_count):
    rows = queries.shape[0]
    span = PAIR * PAIRS_PER_STEP
    steps = queries.shape[1] // span
    zs = devices // 4

    def body(*refs):
        fused_kernel(devices, inverse_count, *refs)

    return pl.pallas_call(
        body,
        grid=(steps,),
        in_specs=[
            pl.BlockSpec(window.shape, lambda i: (0, 0)),
            pl.BlockSpec(start.shape, lambda i: (0, 0)),
            pl.BlockSpec((KV_RANK, span), lambda i: (0, i)),
            pl.BlockSpec((rows, span), lambda i: (0, i)),
        ],
        out_specs=[
            pl.BlockSpec((rows, PAIRS_PER_STEP * 128), lambda i: (0, i)),
            pl.BlockSpec((BLOCK, OUT_WIDTH), lambda i: (0, 0)),
        ],
        out_shape=[
            jax.ShapeDtypeStruct((rows, OUT_WIDTH), jnp.bfloat16),
            jax.ShapeDtypeStruct((BLOCK, OUT_WIDTH), jnp.float32),
        ],
        scratch_shapes=[
            pltpu.VMEM((rows, 2 * BLOCK), jnp.float32),
            pltpu.VMEM((4 * rows, OUT_WIDTH + STRIP - BLOCK), jnp.bfloat16),
            pltpu.VMEM((zs - 1, BLOCK, STRIP), jnp.bfloat16),
            pltpu.VMEM((zs - 1, BLOCK, STRIP), jnp.bfloat16),
            pltpu.VMEM((7, BLOCK, BLOCK), jnp.bfloat16),
            pltpu.VMEM((7, BLOCK, BLOCK), jnp.bfloat16),
            pltpu.SemaphoreType.DMA((steps,)),
            pltpu.SemaphoreType.DMA((steps,)),
            pltpu.SemaphoreType.DMA((steps,)),
            pltpu.SemaphoreType.DMA((steps,)),
            pltpu.SemaphoreType.DMA((steps,)),
            pltpu.SemaphoreType.DMA((steps,)),
            pltpu.SemaphoreType.DMA((zs - 1,)),
            pltpu.SemaphoreType.DMA((zs - 1,)),
            pltpu.SemaphoreType.DMA((7,)),
            pltpu.SemaphoreType.DMA((7,)),
        ],
        compiler_params=pltpu.CompilerParams(
            collective_id=0, has_side_effects=True, vmem_limit_bytes=60 * 1024 * 1024
        ),
    )(window, start, kv_weight, queries)


def per_device(queries, latents, kv_weight, lengths):
    devices = lax.axis_size("dp")
    device = lax.axis_index("dp")
    rows = queries.shape[0]
    inverse_count = 1.0 / (rows * devices)
    halo = lax.ppermute(
        latents[rows - MAXLEN :], "dp", [(source, source + 1) for source in range(devices - 1)]
    )
    window = jnp.concatenate([halo, latents], axis=0)
    rope = window[:, KV_RANK:]
    blank = jnp.zeros((rows + MAXLEN, 2 * (128 - ROPE)), window.dtype)
    window = jnp.concatenate([window, blank, rope], axis=1)

    traces = lengths.shape[0]
    order = jnp.arange(traces, dtype=jnp.int32)
    ends = jnp.sum(jnp.where(order[None, :] <= order[:, None], lengths[None, :], 0), axis=1)
    first_row = device * rows
    position = first_row + jnp.arange(rows, dtype=jnp.int32)
    start = jnp.max(jnp.where(ends[None, :] <= position[:, None], ends[None, :], 0), axis=1)
    start = (start - first_row)[:, None]

    if devices * BLOCK == OUT_WIDTH:
        attn_out, hessian = fused(window, start, kv_weight, queries, devices, inverse_count)
        return attn_out, hessian
    attn_out = attention(window, start, kv_weight, queries)
    partial = lax.dot_general(
        attn_out, attn_out, (((0,), (0,)), ((), ())), preferred_element_type=jnp.float32
    )
    hessian = lax.psum_scatter(partial, "dp", scatter_dimension=0, tiled=True)
    return attn_out, hessian * inverse_count


def solution(mesh):
    placed = (P(("rep", "dp"), None), P(("rep", "dp"), None), P(), P("rep"))
    return jax.shard_map(
        per_device,
        mesh=mesh,
        in_specs=placed,
        out_specs=(P(("rep", "dp"), None), P(("rep", "dp"), None)),
        check_vma=False,
    )
```

```python
import math

import jax
import jax.numpy as jnp
from jax import lax
from jax.experimental import pallas as pl
from jax.experimental.pallas import tpu as pltpu
from jax.sharding import PartitionSpec as P

HEADS = 32
NOPE = 128
ROPE = 64
V_DIM = 64
KV_RANK = 512
MAXLEN = 128
OUT_WIDTH = 2048

MASKED = -1e30
BLOCK = 128
HEAD_WIDTH = NOPE + ROPE
PAIR = 2 * HEAD_WIDTH
PAIRS_PER_STEP = 1
STRIP = 9 * BLOCK
LAG = 2
HALVES = 2
HALF = BLOCK // HALVES
MESH = pl.DeviceIdType.MESH
EXP_SCALE = math.log2(math.e) / math.sqrt(NOPE + ROPE)


def attention_kernel(window_ref, start_ref, weight_ref, query_ref, out_ref, bias_ref):
    rows = query_ref.shape[0]
    blocks = rows // BLOCK

    @pl.when(pl.program_id(0) == 0)
    def _():
        for b in range(blocks):
            start = start_ref[b * BLOCK : (b + 1) * BLOCK, :]
            key = lax.broadcasted_iota(jnp.int32, (BLOCK, 2 * BLOCK), 1) + (b - 1) * BLOCK
            query = lax.broadcasted_iota(jnp.int32, (BLOCK, 2 * BLOCK), 0) + b * BLOCK
            allowed = (key <= query) & (key >= start)
            bias_ref[b * BLOCK : (b + 1) * BLOCK, :] = jnp.where(allowed, 0.0, MASKED)

    content = window_ref[:, :KV_RANK]
    rope_low = window_ref[:, KV_RANK : KV_RANK + 128]
    rope_high = window_ref[:, KV_RANK + 128 :]
    keys_rows = window_ref.shape[0]
    low = lax.broadcasted_iota(jnp.int32, (keys_rows, 128), 1) < 64
    low_out = lax.broadcasted_iota(jnp.int32, (BLOCK, 128), 1) < 64
    one = jnp.ones((keys_rows, 128), jnp.bfloat16)
    zero = jnp.zeros((keys_rows, 128), jnp.bfloat16)
    for pair in range(PAIRS_PER_STEP):
        at = pair * PAIR
        kv = jnp.dot(
            content, weight_ref[:, at : at + PAIR], preferred_element_type=jnp.float32
        ).astype(jnp.bfloat16)
        first, second, third = kv[:, :128], kv[:, 128:256], kv[:, 256:384]
        keys = (
            jnp.concatenate([first, rope_low], axis=1),
            jnp.concatenate(
                [jnp.where(low, zero, second), jnp.where(low, third, rope_high)], axis=1
            ),
        )
        values = (jnp.where(low, second, one), jnp.where(low, one, third))
        for b in range(blocks):
            rows_at = slice(b * BLOCK, (b + 1) * BLOCK)
            keys_at = slice(b * BLOCK, (b + 2) * BLOCK)
            bias = bias_ref[rows_at, :]
            mixed = []
            for head in range(2):
                query = query_ref[rows_at, at + head * 128 : at + head * 128 + 256]
                scores = lax.dot_general(
                    query,
                    keys[head][keys_at],
                    (((1,), (1,)), ((), ())),
                    preferred_element_type=jnp.float32,
                )
                scores = scores + bias
                top = jnp.max(scores, axis=1, keepdims=True)
                weights = jnp.exp2((scores - top) * EXP_SCALE).astype(jnp.bfloat16)
                mixed.append(
                    jnp.dot(weights, values[head][keys_at], preferred_element_type=jnp.float32)
                )
            total = pltpu.roll(jnp.where(low_out, mixed[1], mixed[0]), 64, 1)
            result = jnp.where(low_out, mixed[0], mixed[1]) / total
            out_ref[rows_at, pair * 128 : (pair + 1) * 128] = result.astype(jnp.bfloat16)


def attention(window, start, kv_weight, queries):
    rows = queries.shape[0]
    span = PAIR * PAIRS_PER_STEP
    return pl.pallas_call(
        attention_kernel,
        grid=(queries.shape[1] // span,),
        in_specs=[
            pl.BlockSpec(window.shape, lambda i: (0, 0)),
            pl.BlockSpec(start.shape, lambda i: (0, 0)),
            pl.BlockSpec((KV_RANK, span), lambda i: (0, i)),
            pl.BlockSpec((rows, span), lambda i: (0, i)),
        ],
        out_specs=pl.BlockSpec((rows, PAIRS_PER_STEP * 128), lambda i: (0, i)),
        out_shape=jax.ShapeDtypeStruct((rows, OUT_WIDTH), jnp.bfloat16),
        scratch_shapes=[pltpu.VMEM((rows, 2 * BLOCK), jnp.float32)],
        compiler_params=pltpu.CompilerParams(vmem_limit_bytes=40 * 1024 * 1024),
    )(window, start, kv_weight, queries)


def fused_kernel(
    devices,
    inverse_count,
    window_ref,
    start_ref,
    weight_ref,
    query_ref,
    out_ref,
    hessian_ref,
    bias_ref,
    a_all,
    acc,
    z_send,
    z_recv,
    t_send,
    t_recv,
    pair_send_sem,
    pair_recv_sem,
    y_send_sem,
    y_recv_sem,
    pass_send_sem,
    pass_recv_sem,
    z_send_sem,
    z_recv_sem,
    t_send_sem,
    t_recv_sem,
):
    rows = query_ref.shape[0]
    width = out_ref.shape[1]
    steps = OUT_WIDTH // width
    step = pl.program_id(0)
    me = lax.axis_index("dp")
    rep = lax.axis_index("rep")
    core = lax.rem(me, 2)
    y = lax.rem(me // 2, 2)
    z = me // 4

    def index_of(z_at, y_at, core_at):
        return (z_at * 2 + y_at) * 2 + core_at

    def other(k):
        return lax.rem(me + k, devices)

    partner = index_of(z, y, 1 - core)
    across = index_of(z, 1 - y, core)

    def piece_copy(source, target, piece, send_sem, recv_sem, device):
        at = pl.ds(pl.multiple_of(piece * width, width), width)
        return pltpu.make_async_remote_copy(
            src_ref=a_all.at[source * rows : (source + 1) * rows, at],
            dst_ref=a_all.at[target * rows : (target + 1) * rows, at],
            send_sem=send_sem.at[piece],
            recv_sem=recv_sem.at[piece],
            device_id=(rep, device),
            device_id_type=MESH,
        )

    def pair_copy(piece):
        return piece_copy(0, 1, piece, pair_send_sem, pair_recv_sem, partner)

    def y_copy(piece):
        return piece_copy(0, 2, piece, y_send_sem, y_recv_sem, across)

    def pass_copy(piece):
        return piece_copy(2, 3, piece, pass_send_sem, pass_recv_sem, partner)

    @pl.when(step == 0)
    def _():
        barrier = pltpu.get_barrier_semaphore()
        for k in range(1, devices):
            pl.semaphore_signal(barrier, inc=1, device_id=(rep, other(k)), device_id_type=MESH)

    attention_kernel(window_ref, start_ref, weight_ref, query_ref, out_ref, bias_ref)
    a_all[0:rows, pl.ds(pl.multiple_of(step * width, width), width)] = out_ref[...]

    @pl.when(step == 0)
    def _():
        pl.semaphore_wait(pltpu.get_barrier_semaphore(), devices - 1)

    y_copy(step).start()
    pair_copy(step).start()

    @pl.when(step >= LAG)
    def _():
        y_copy(step - LAG).wait_recv()
        pass_copy(step - LAG).start()

    @pl.when(step == steps - 1)
    def _():
        z_low, z_high = lax.rem(z, 2), z // 2
        beside = index_of(z_high * 2 + 1 - z_low, y, core)
        beyond = index_of((1 - z_high) * 2 + z_low, y, core)
        owners = (index_of((1 - z_high) * 2 + 1 - z_low, y, core), beside, beyond, me)

        def strip(owner, first, last):
            at = pl.multiple_of(owner * BLOCK, BLOCK)
            return lax.dot_general(
                a_all[first * rows : last * rows, pl.ds(at, BLOCK)],
                a_all[first * rows : last * rows, pl.ds(at, STRIP)],
                (((0,), (0,)), ((), ())),
                preferred_element_type=jnp.float32,
            )

        def wrap(first, last):
            a_all[first * rows : last * rows, OUT_WIDTH:] = a_all[
                first * rows : last * rows, : STRIP - BLOCK
            ]

        def z_copy(j, half, device):
            at = slice(half * HALF, (half + 1) * HALF)
            return pltpu.make_async_remote_copy(
                src_ref=z_send.at[j, at],
                dst_ref=z_recv.at[j, at],
                send_sem=z_send_sem.at[j * HALVES + half],
                recv_sem=z_recv_sem.at[j * HALVES + half],
                device_id=(rep, device),
                device_id_type=MESH,
            )

        def forward(piece):
            y_copy(piece).wait_recv()
            pass_copy(piece).start()

        for piece in range(steps):
            pair_copy(piece).wait_recv()
        wrap(0, 2)
        for j in range(4):
            acc[j] = strip(owners[j], 0, 2)
            if j % 2 == 1:
                forward(steps - 2 + j // 2)
        wrap(2, 3)
        acc[0] = acc[0] + strip(owners[0], 2, 3)
        for piece in range(steps):
            pass_copy(piece).wait_recv()
        wrap(3, 4)
        z_send[0] = (acc[0] + strip(owners[0], 3, 4)).astype(jnp.bfloat16)
        for half in range(HALVES):
            z_copy(0, half, beside).start()
        z_send[1] = (acc[1] + strip(owners[1], 2, 4)).astype(jnp.bfloat16)
        for half in range(HALVES):
            z_copy(1, half, beside).start()
        acc[2] = acc[2] + strip(owners[2], 2, 4)
        acc[3] = acc[3] + strip(owners[3], 2, 4)
        for half in range(HALVES):
            at = slice(half * HALF, (half + 1) * HALF)
            z_copy(0, half, beside).wait_recv()
            z_send[2, at] = (acc[2, at] + z_recv[0, at].astype(jnp.float32)).astype(jnp.bfloat16)
            z_copy(2, half, beyond).start()
        for half in range(HALVES):
            z_copy(1, half, beside).wait_recv()
        total = acc[3] + z_recv[1].astype(jnp.float32)
        for half in range(HALVES):
            z_copy(2, half, beyond).wait_recv()
        total = total + z_recv[2].astype(jnp.float32)
        total = total * inverse_count

        t_copies = []
        for k in range(1, 8):
            t_send[k - 1] = total[:, k * BLOCK : (k + 1) * BLOCK].T.astype(jnp.bfloat16)
            copy = pltpu.make_async_remote_copy(
                src_ref=t_send.at[k - 1],
                dst_ref=t_recv.at[k - 1],
                send_sem=t_send_sem.at[k - 1],
                recv_sem=t_recv_sem.at[k - 1],
                device_id=(rep, other(k)),
                device_id_type=MESH,
            )
            copy.start()
            t_copies.append(copy)
        for k in range(9):
            at = pl.multiple_of(other(k) * BLOCK, BLOCK)
            hessian_ref[:, pl.ds(at, BLOCK)] = total[:, k * BLOCK : (k + 1) * BLOCK]
        for k in range(1, 8):
            t_copies[k - 1].wait_recv()
            at = pl.multiple_of(other(devices - k) * BLOCK, BLOCK)
            hessian_ref[:, pl.ds(at, BLOCK)] = t_recv[k - 1].astype(jnp.float32)
        for piece in range(steps):
            pair_copy(piece).wait_send()
            y_copy(piece).wait_send()
            pass_copy(piece).wait_send()
        for half in range(HALVES):
            z_copy(0, half, beside).wait_send()
            z_copy(1, half, beside).wait_send()
            z_copy(2, half, beyond).wait_send()
        for copy in t_copies:
            copy.wait_send()


def fused(window, start, kv_weight, queries, devices, inverse_count):
    rows = queries.shape[0]
    span = PAIR * PAIRS_PER_STEP
    steps = queries.shape[1] // span

    def body(*refs):
        fused_kernel(devices, inverse_count, *refs)

    return pl.pallas_call(
        body,
        grid=(steps,),
        in_specs=[
            pl.BlockSpec(window.shape, lambda i: (0, 0)),
            pl.BlockSpec(start.shape, lambda i: (0, 0)),
            pl.BlockSpec((KV_RANK, span), lambda i: (0, i)),
            pl.BlockSpec((rows, span), lambda i: (0, i)),
        ],
        out_specs=[
            pl.BlockSpec((rows, PAIRS_PER_STEP * 128), lambda i: (0, i)),
            pl.BlockSpec((BLOCK, OUT_WIDTH), lambda i: (0, 0)),
        ],
        out_shape=[
            jax.ShapeDtypeStruct((rows, OUT_WIDTH), jnp.bfloat16),
            jax.ShapeDtypeStruct((BLOCK, OUT_WIDTH), jnp.float32),
        ],
        scratch_shapes=[
            pltpu.VMEM((rows, 2 * BLOCK), jnp.float32),
            pltpu.VMEM((4 * rows, OUT_WIDTH + STRIP - BLOCK), jnp.bfloat16),
            pltpu.VMEM((4, BLOCK, STRIP), jnp.float32),
            pltpu.VMEM((3, BLOCK, STRIP), jnp.bfloat16),
            pltpu.VMEM((3, BLOCK, STRIP), jnp.bfloat16),
            pltpu.VMEM((7, BLOCK, BLOCK), jnp.bfloat16),
            pltpu.VMEM((7, BLOCK, BLOCK), jnp.bfloat16),
            pltpu.SemaphoreType.DMA((steps,)),
            pltpu.SemaphoreType.DMA((steps,)),
            pltpu.SemaphoreType.DMA((steps,)),
            pltpu.SemaphoreType.DMA((steps,)),
            pltpu.SemaphoreType.DMA((steps,)),
            pltpu.SemaphoreType.DMA((steps,)),
            pltpu.SemaphoreType.DMA((3 * HALVES,)),
            pltpu.SemaphoreType.DMA((3 * HALVES,)),
            pltpu.SemaphoreType.DMA((7,)),
            pltpu.SemaphoreType.DMA((7,)),
        ],
        compiler_params=pltpu.CompilerParams(
            collective_id=0, has_side_effects=True, vmem_limit_bytes=60 * 1024 * 1024
        ),
    )(window, start, kv_weight, queries)


def per_device(queries, latents, kv_weight, lengths):
    devices = lax.axis_size("dp")
    device = lax.axis_index("dp")
    rows = queries.shape[0]
    inverse_count = 1.0 / (rows * devices)
    halo = lax.ppermute(
        latents[rows - MAXLEN :], "dp", [(source, source + 1) for source in range(devices - 1)]
    )
    window = jnp.concatenate([halo, latents], axis=0)
    rope = window[:, KV_RANK:]
    blank = jnp.zeros((rows + MAXLEN, 2 * (128 - ROPE)), window.dtype)
    window = jnp.concatenate([window, blank, rope], axis=1)

    traces = lengths.shape[0]
    order = jnp.arange(traces, dtype=jnp.int32)
    ends = jnp.sum(jnp.where(order[None, :] <= order[:, None], lengths[None, :], 0), axis=1)
    first_row = device * rows
    position = first_row + jnp.arange(rows, dtype=jnp.int32)
    start = jnp.max(jnp.where(ends[None, :] <= position[:, None], ends[None, :], 0), axis=1)
    start = (start - first_row)[:, None]

    if devices == 16:
        attn_out, hessian = fused(window, start, kv_weight, queries, devices, inverse_count)
        return attn_out, hessian
    attn_out = attention(window, start, kv_weight, queries)
    partial = lax.dot_general(
        attn_out, attn_out, (((0,), (0,)), ((), ())), preferred_element_type=jnp.float32
    )
    hessian = lax.psum_scatter(partial, "dp", scatter_dimension=0, tiled=True)
    return attn_out, hessian * inverse_count


def solution(mesh):
    placed = (P(("rep", "dp"), None), P(("rep", "dp"), None), P(), P("rep"))
    return jax.shard_map(
        per_device,
        mesh=mesh,
        in_specs=placed,
        out_specs=(P(("rep", "dp"), None), P(("rep", "dp"), None)),
        check_vma=False,
    )
```

```python
import math

import jax
import jax.numpy as jnp
from jax import lax
from jax.experimental import pallas as pl
from jax.experimental.pallas import tpu as pltpu
from jax.sharding import PartitionSpec as P

HEADS = 32
NOPE = 128
ROPE = 64
V_DIM = 64
KV_RANK = 512
MAXLEN = 128
OUT_WIDTH = 2048

MASKED = -1e30
BLOCK = 128
HEAD_WIDTH = NOPE + ROPE
PAIR = 2 * HEAD_WIDTH
PAIRS_PER_STEP = 1
STRIP = 9 * BLOCK
LAG = 2
HALVES = 2
CUTS = (0, 5 * BLOCK, STRIP)
MESH = pl.DeviceIdType.MESH
EXP_SCALE = math.log2(math.e) / math.sqrt(NOPE + ROPE)


def attention_kernel(window_ref, start_ref, weight_ref, query_ref, out_ref, bias_ref):
    rows = query_ref.shape[0]
    blocks = rows // BLOCK

    @pl.when(pl.program_id(0) == 0)
    def _():
        for b in range(blocks):
            start = start_ref[b * BLOCK : (b + 1) * BLOCK, :]
            key = lax.broadcasted_iota(jnp.int32, (BLOCK, 2 * BLOCK), 1) + (b - 1) * BLOCK
            query = lax.broadcasted_iota(jnp.int32, (BLOCK, 2 * BLOCK), 0) + b * BLOCK
            allowed = (key <= query) & (key >= start)
            bias_ref[b * BLOCK : (b + 1) * BLOCK, :] = jnp.where(allowed, 0.0, MASKED)

    content = window_ref[:, :KV_RANK]
    rope_low = window_ref[:, KV_RANK : KV_RANK + 128]
    rope_high = window_ref[:, KV_RANK + 128 :]
    keys_rows = window_ref.shape[0]
    low = lax.broadcasted_iota(jnp.int32, (keys_rows, 128), 1) < 64
    low_out = lax.broadcasted_iota(jnp.int32, (BLOCK, 128), 1) < 64
    one = jnp.ones((keys_rows, 128), jnp.bfloat16)
    zero = jnp.zeros((keys_rows, 128), jnp.bfloat16)
    for pair in range(PAIRS_PER_STEP):
        at = pair * PAIR
        kv = jnp.dot(
            content, weight_ref[:, at : at + PAIR], preferred_element_type=jnp.float32
        ).astype(jnp.bfloat16)
        first, second, third = kv[:, :128], kv[:, 128:256], kv[:, 256:384]
        keys = (
            jnp.concatenate([first, rope_low], axis=1),
            jnp.concatenate(
                [jnp.where(low, zero, second), jnp.where(low, third, rope_high)], axis=1
            ),
        )
        values = (jnp.where(low, second, one), jnp.where(low, one, third))
        for b in range(blocks):
            rows_at = slice(b * BLOCK, (b + 1) * BLOCK)
            keys_at = slice(b * BLOCK, (b + 2) * BLOCK)
            bias = bias_ref[rows_at, :]
            mixed = []
            for head in range(2):
                query = query_ref[rows_at, at + head * 128 : at + head * 128 + 256]
                scores = lax.dot_general(
                    query,
                    keys[head][keys_at],
                    (((1,), (1,)), ((), ())),
                    preferred_element_type=jnp.float32,
                )
                scores = scores + bias
                top = jnp.max(scores, axis=1, keepdims=True)
                weights = jnp.exp2((scores - top) * EXP_SCALE).astype(jnp.bfloat16)
                mixed.append(
                    jnp.dot(weights, values[head][keys_at], preferred_element_type=jnp.float32)
                )
            total = pltpu.roll(jnp.where(low_out, mixed[1], mixed[0]), 64, 1)
            result = jnp.where(low_out, mixed[0], mixed[1]) / total
            out_ref[rows_at, pair * 128 : (pair + 1) * 128] = result.astype(jnp.bfloat16)


def attention(window, start, kv_weight, queries):
    rows = queries.shape[0]
    span = PAIR * PAIRS_PER_STEP
    return pl.pallas_call(
        attention_kernel,
        grid=(queries.shape[1] // span,),
        in_specs=[
            pl.BlockSpec(window.shape, lambda i: (0, 0)),
            pl.BlockSpec(start.shape, lambda i: (0, 0)),
            pl.BlockSpec((KV_RANK, span), lambda i: (0, i)),
            pl.BlockSpec((rows, span), lambda i: (0, i)),
        ],
        out_specs=pl.BlockSpec((rows, PAIRS_PER_STEP * 128), lambda i: (0, i)),
        out_shape=jax.ShapeDtypeStruct((rows, OUT_WIDTH), jnp.bfloat16),
        scratch_shapes=[pltpu.VMEM((rows, 2 * BLOCK), jnp.float32)],
        compiler_params=pltpu.CompilerParams(vmem_limit_bytes=40 * 1024 * 1024),
    )(window, start, kv_weight, queries)


def fused_kernel(
    devices,
    inverse_count,
    window_ref,
    start_ref,
    weight_ref,
    query_ref,
    out_ref,
    hessian_ref,
    bias_ref,
    a_all,
    acc,
    z_send,
    z_recv,
    t_send,
    t_recv,
    pair_send_sem,
    pair_recv_sem,
    y_send_sem,
    y_recv_sem,
    pass_send_sem,
    pass_recv_sem,
    z_send_sem,
    z_recv_sem,
    t_send_sem,
    t_recv_sem,
):
    rows = query_ref.shape[0]
    width = out_ref.shape[1]
    steps = OUT_WIDTH // width
    step = pl.program_id(0)
    me = lax.axis_index("dp")
    rep = lax.axis_index("rep")
    core = lax.rem(me, 2)
    y = lax.rem(me // 2, 2)
    z = me // 4

    def index_of(z_at, y_at, core_at):
        return (z_at * 2 + y_at) * 2 + core_at

    def other(k):
        return lax.rem(me + k, devices)

    partner = index_of(z, y, 1 - core)
    across = index_of(z, 1 - y, core)

    def piece_copy(source, target, piece, send_sem, recv_sem, device):
        at = pl.ds(pl.multiple_of(piece * width, width), width)
        return pltpu.make_async_remote_copy(
            src_ref=a_all.at[source * rows : (source + 1) * rows, at],
            dst_ref=a_all.at[target * rows : (target + 1) * rows, at],
            send_sem=send_sem.at[piece],
            recv_sem=recv_sem.at[piece],
            device_id=(rep, device),
            device_id_type=MESH,
        )

    def pair_copy(piece):
        return piece_copy(0, 1, piece, pair_send_sem, pair_recv_sem, partner)

    def y_copy(piece):
        return piece_copy(0, 2, piece, y_send_sem, y_recv_sem, across)

    def pass_copy(piece):
        return piece_copy(2, 3, piece, pass_send_sem, pass_recv_sem, partner)

    @pl.when(step == 0)
    def _():
        barrier = pltpu.get_barrier_semaphore()
        for k in range(1, devices):
            pl.semaphore_signal(barrier, inc=1, device_id=(rep, other(k)), device_id_type=MESH)

    attention_kernel(window_ref, start_ref, weight_ref, query_ref, out_ref, bias_ref)
    a_all[0:rows, pl.ds(pl.multiple_of(step * width, width), width)] = out_ref[...]

    @pl.when(step == 0)
    def _():
        pl.semaphore_wait(pltpu.get_barrier_semaphore(), devices - 1)

    y_copy(step).start()
    pair_copy(step).start()

    @pl.when(step >= LAG)
    def _():
        y_copy(step - LAG).wait_recv()
        pass_copy(step - LAG).start()

    @pl.when(step == steps - 1)
    def _():
        z_low, z_high = lax.rem(z, 2), z // 2
        beside = index_of(z_high * 2 + 1 - z_low, y, core)
        beyond = index_of((1 - z_high) * 2 + z_low, y, core)
        owners = (index_of((1 - z_high) * 2 + 1 - z_low, y, core), beside, beyond, me)

        def strip(owner, first, last):
            at = pl.multiple_of(owner * BLOCK, BLOCK)
            return lax.dot_general(
                a_all[first * rows : last * rows, pl.ds(at, BLOCK)],
                a_all[first * rows : last * rows, pl.ds(at, STRIP)],
                (((0,), (0,)), ((), ())),
                preferred_element_type=jnp.float32,
            )

        def wrap(first, last):
            a_all[first * rows : last * rows, OUT_WIDTH:] = a_all[
                first * rows : last * rows, : STRIP - BLOCK
            ]

        def z_copy(j, half, device):
            at = slice(CUTS[half], CUTS[half + 1])
            return pltpu.make_async_remote_copy(
                src_ref=z_send.at[j, :, at],
                dst_ref=z_recv.at[j, :, at],
                send_sem=z_send_sem.at[j * HALVES + half],
                recv_sem=z_recv_sem.at[j * HALVES + half],
                device_id=(rep, device),
                device_id_type=MESH,
            )

        def forward(piece):
            y_copy(piece).wait_recv()
            pass_copy(piece).start()

        for piece in range(steps):
            pair_copy(piece).wait_recv()
        wrap(0, 2)
        for j in range(4):
            acc[j] = strip(owners[j], 0, 2)
            if j % 2 == 1:
                forward(steps - 2 + j // 2)
        wrap(2, 3)
        acc[0] = acc[0] + strip(owners[0], 2, 3)
        for piece in range(steps):
            pass_copy(piece).wait_recv()
        wrap(3, 4)
        z_send[0] = (acc[0] + strip(owners[0], 3, 4)).astype(jnp.bfloat16)
        for half in range(HALVES):
            z_copy(0, half, beside).start()
        z_send[1] = (acc[1] + strip(owners[1], 2, 4)).astype(jnp.bfloat16)
        for half in range(HALVES):
            z_copy(1, half, beside).start()
        acc[2] = acc[2] + strip(owners[2], 2, 4)
        acc[3] = acc[3] + strip(owners[3], 2, 4)
        for half in range(HALVES):
            at = slice(CUTS[half], CUTS[half + 1])
            z_copy(0, half, beside).wait_recv()
            z_send[2, :, at] = (acc[2, :, at] + z_recv[0, :, at].astype(jnp.float32)).astype(jnp.bfloat16)
            z_copy(2, half, beyond).start()
        t_copies = []
        for half in range(HALVES):
            at = slice(CUTS[half], CUTS[half + 1])
            z_copy(1, half, beside).wait_recv()
            total = acc[3, :, at] + z_recv[1, :, at].astype(jnp.float32)
            z_copy(2, half, beyond).wait_recv()
            acc[3, :, at] = (total + z_recv[2, :, at].astype(jnp.float32)) * inverse_count
            for k in range(max(1, CUTS[half] // BLOCK), min(8, CUTS[half + 1] // BLOCK)):
                t_send[k - 1] = acc[3, :, k * BLOCK : (k + 1) * BLOCK].T.astype(jnp.bfloat16)
                copy = pltpu.make_async_remote_copy(
                    src_ref=t_send.at[k - 1],
                    dst_ref=t_recv.at[k - 1],
                    send_sem=t_send_sem.at[k - 1],
                    recv_sem=t_recv_sem.at[k - 1],
                    device_id=(rep, other(k)),
                    device_id_type=MESH,
                )
                copy.start()
                t_copies.append(copy)
        for k in range(9):
            at = pl.multiple_of(other(k) * BLOCK, BLOCK)
            hessian_ref[:, pl.ds(at, BLOCK)] = acc[3, :, k * BLOCK : (k + 1) * BLOCK]
        for k in range(1, 8):
            t_copies[k - 1].wait_recv()
            at = pl.multiple_of(other(devices - k) * BLOCK, BLOCK)
            hessian_ref[:, pl.ds(at, BLOCK)] = t_recv[k - 1].astype(jnp.float32)
        for piece in range(steps):
            pair_copy(piece).wait_send()
            y_copy(piece).wait_send()
            pass_copy(piece).wait_send()
        for half in range(HALVES):
            z_copy(0, half, beside).wait_send()
            z_copy(1, half, beside).wait_send()
            z_copy(2, half, beyond).wait_send()
        for copy in t_copies:
            copy.wait_send()


def fused(window, start, kv_weight, queries, devices, inverse_count):
    rows = queries.shape[0]
    span = PAIR * PAIRS_PER_STEP
    steps = queries.shape[1] // span

    def body(*refs):
        fused_kernel(devices, inverse_count, *refs)

    return pl.pallas_call(
        body,
        grid=(steps,),
        in_specs=[
            pl.BlockSpec(window.shape, lambda i: (0, 0)),
            pl.BlockSpec(start.shape, lambda i: (0, 0)),
            pl.BlockSpec((KV_RANK, span), lambda i: (0, i)),
            pl.BlockSpec((rows, span), lambda i: (0, i)),
        ],
        out_specs=[
            pl.BlockSpec((rows, PAIRS_PER_STEP * 128), lambda i: (0, i)),
            pl.BlockSpec((BLOCK, OUT_WIDTH), lambda i: (0, 0)),
        ],
        out_shape=[
            jax.ShapeDtypeStruct((rows, OUT_WIDTH), jnp.bfloat16),
            jax.ShapeDtypeStruct((BLOCK, OUT_WIDTH), jnp.float32),
        ],
        scratch_shapes=[
            pltpu.VMEM((rows, 2 * BLOCK), jnp.float32),
            pltpu.VMEM((4 * rows, OUT_WIDTH + STRIP - BLOCK), jnp.bfloat16),
            pltpu.VMEM((4, BLOCK, STRIP), jnp.float32),
            pltpu.VMEM((3, BLOCK, STRIP), jnp.bfloat16),
            pltpu.VMEM((3, BLOCK, STRIP), jnp.bfloat16),
            pltpu.VMEM((7, BLOCK, BLOCK), jnp.bfloat16),
            pltpu.VMEM((7, BLOCK, BLOCK), jnp.bfloat16),
            pltpu.SemaphoreType.DMA((steps,)),
            pltpu.SemaphoreType.DMA((steps,)),
            pltpu.SemaphoreType.DMA((steps,)),
            pltpu.SemaphoreType.DMA((steps,)),
            pltpu.SemaphoreType.DMA((steps,)),
            pltpu.SemaphoreType.DMA((steps,)),
            pltpu.SemaphoreType.DMA((3 * HALVES,)),
            pltpu.SemaphoreType.DMA((3 * HALVES,)),
            pltpu.SemaphoreType.DMA((7,)),
            pltpu.SemaphoreType.DMA((7,)),
        ],
        compiler_params=pltpu.CompilerParams(
            collective_id=0, has_side_effects=True, vmem_limit_bytes=60 * 1024 * 1024
        ),
    )(window, start, kv_weight, queries)


def per_device(queries, latents, kv_weight, lengths):
    devices = lax.axis_size("dp")
    device = lax.axis_index("dp")
    rows = queries.shape[0]
    inverse_count = 1.0 / (rows * devices)
    halo = lax.ppermute(
        latents[rows - MAXLEN :], "dp", [(source, source + 1) for source in range(devices - 1)]
    )
    window = jnp.concatenate([halo, latents], axis=0)
    rope = window[:, KV_RANK:]
    blank = jnp.zeros((rows + MAXLEN, 2 * (128 - ROPE)), window.dtype)
    window = jnp.concatenate([window, blank, rope], axis=1)

    traces = lengths.shape[0]
    order = jnp.arange(traces, dtype=jnp.int32)
    ends = jnp.sum(jnp.where(order[None, :] <= order[:, None], lengths[None, :], 0), axis=1)
    first_row = device * rows
    position = first_row + jnp.arange(rows, dtype=jnp.int32)
    start = jnp.max(jnp.where(ends[None, :] <= position[:, None], ends[None, :], 0), axis=1)
    start = (start - first_row)[:, None]

    if devices == 16:
        attn_out, hessian = fused(window, start, kv_weight, queries, devices, inverse_count)
        return attn_out, hessian
    attn_out = attention(window, start, kv_weight, queries)
    partial = lax.dot_general(
        attn_out, attn_out, (((0,), (0,)), ((), ())), preferred_element_type=jnp.float32
    )
    hessian = lax.psum_scatter(partial, "dp", scatter_dimension=0, tiled=True)
    return attn_out, hessian * inverse_count


def solution(mesh):
    placed = (P(("rep", "dp"), None), P(("rep", "dp"), None), P(), P("rep"))
    return jax.shard_map(
        per_device,
        mesh=mesh,
        in_specs=placed,
        out_specs=(P(("rep", "dp"), None), P(("rep", "dp"), None)),
        check_vma=False,
    )
```

```python
import math

import jax
import jax.numpy as jnp
from jax import lax
from jax.experimental import pallas as pl
from jax.experimental.pallas import tpu as pltpu
from jax.sharding import PartitionSpec as P

HEADS = 32
NOPE = 128
ROPE = 64
V_DIM = 64
KV_RANK = 512
MAXLEN = 128
OUT_WIDTH = 2048

MASKED = -1e30
BLOCK = 128
HEAD_WIDTH = NOPE + ROPE
PAIR = 2 * HEAD_WIDTH
PAIRS_PER_STEP = 1
STRIP = 9 * BLOCK
LAG = 2
HALVES = 3
CUTS = (0, 3 * BLOCK, 6 * BLOCK, STRIP)
MESH = pl.DeviceIdType.MESH
EXP_SCALE = math.log2(math.e) / math.sqrt(NOPE + ROPE)


def attention_kernel(window_ref, start_ref, weight_ref, query_ref, out_ref, bias_ref):
    rows = query_ref.shape[0]
    blocks = rows // BLOCK

    @pl.when(pl.program_id(0) == 0)
    def _():
        for b in range(blocks):
            start = start_ref[b * BLOCK : (b + 1) * BLOCK, :]
            key = lax.broadcasted_iota(jnp.int32, (BLOCK, 2 * BLOCK), 1) + (b - 1) * BLOCK
            query = lax.broadcasted_iota(jnp.int32, (BLOCK, 2 * BLOCK), 0) + b * BLOCK
            allowed = (key <= query) & (key >= start)
            bias_ref[b * BLOCK : (b + 1) * BLOCK, :] = jnp.where(allowed, 0.0, MASKED)

    content = window_ref[:, :KV_RANK]
    rope_low = window_ref[:, KV_RANK : KV_RANK + 128]
    rope_high = window_ref[:, KV_RANK + 128 :]
    keys_rows = window_ref.shape[0]
    low = lax.broadcasted_iota(jnp.int32, (keys_rows, 128), 1) < 64
    low_out = lax.broadcasted_iota(jnp.int32, (BLOCK, 128), 1) < 64
    one = jnp.ones((keys_rows, 128), jnp.bfloat16)
    zero = jnp.zeros((keys_rows, 128), jnp.bfloat16)
    for pair in range(PAIRS_PER_STEP):
        at = pair * PAIR
        kv = jnp.dot(
            content, weight_ref[:, at : at + PAIR], preferred_element_type=jnp.float32
        ).astype(jnp.bfloat16)
        first, second, third = kv[:, :128], kv[:, 128:256], kv[:, 256:384]
        keys = (
            jnp.concatenate([first, rope_low], axis=1),
            jnp.concatenate(
                [jnp.where(low, zero, second), jnp.where(low, third, rope_high)], axis=1
            ),
        )
        values = (jnp.where(low, second, one), jnp.where(low, one, third))
        for b in range(blocks):
            rows_at = slice(b * BLOCK, (b + 1) * BLOCK)
            keys_at = slice(b * BLOCK, (b + 2) * BLOCK)
            bias = bias_ref[rows_at, :]
            mixed = []
            for head in range(2):
                query = query_ref[rows_at, at + head * 128 : at + head * 128 + 256]
                scores = lax.dot_general(
                    query,
                    keys[head][keys_at],
                    (((1,), (1,)), ((), ())),
                    preferred_element_type=jnp.float32,
                )
                scores = scores + bias
                top = jnp.max(scores, axis=1, keepdims=True)
                weights = jnp.exp2((scores - top) * EXP_SCALE).astype(jnp.bfloat16)
                mixed.append(
                    jnp.dot(weights, values[head][keys_at], preferred_element_type=jnp.float32)
                )
            total = pltpu.roll(jnp.where(low_out, mixed[1], mixed[0]), 64, 1)
            result = jnp.where(low_out, mixed[0], mixed[1]) / total
            out_ref[rows_at, pair * 128 : (pair + 1) * 128] = result.astype(jnp.bfloat16)


def attention(window, start, kv_weight, queries):
    rows = queries.shape[0]
    span = PAIR * PAIRS_PER_STEP
    return pl.pallas_call(
        attention_kernel,
        grid=(queries.shape[1] // span,),
        in_specs=[
            pl.BlockSpec(window.shape, lambda i: (0, 0)),
            pl.BlockSpec(start.shape, lambda i: (0, 0)),
            pl.BlockSpec((KV_RANK, span), lambda i: (0, i)),
            pl.BlockSpec((rows, span), lambda i: (0, i)),
        ],
        out_specs=pl.BlockSpec((rows, PAIRS_PER_STEP * 128), lambda i: (0, i)),
        out_shape=jax.ShapeDtypeStruct((rows, OUT_WIDTH), jnp.bfloat16),
        scratch_shapes=[pltpu.VMEM((rows, 2 * BLOCK), jnp.float32)],
        compiler_params=pltpu.CompilerParams(vmem_limit_bytes=40 * 1024 * 1024),
    )(window, start, kv_weight, queries)


def fused_kernel(
    devices,
    inverse_count,
    window_ref,
    start_ref,
    weight_ref,
    query_ref,
    out_ref,
    hessian_ref,
    bias_ref,
    a_all,
    acc,
    z_send,
    z_recv,
    t_send,
    t_recv,
    pair_send_sem,
    pair_recv_sem,
    y_send_sem,
    y_recv_sem,
    pass_send_sem,
    pass_recv_sem,
    z_send_sem,
    z_recv_sem,
    t_send_sem,
    t_recv_sem,
):
    rows = query_ref.shape[0]
    width = out_ref.shape[1]
    steps = OUT_WIDTH // width
    step = pl.program_id(0)
    me = lax.axis_index("dp")
    rep = lax.axis_index("rep")
    core = lax.rem(me, 2)
    y = lax.rem(me // 2, 2)
    z = me // 4

    def index_of(z_at, y_at, core_at):
        return (z_at * 2 + y_at) * 2 + core_at

    def other(k):
        return lax.rem(me + k, devices)

    partner = index_of(z, y, 1 - core)
    across = index_of(z, 1 - y, core)

    def piece_copy(source, target, piece, send_sem, recv_sem, device):
        at = pl.ds(pl.multiple_of(piece * width, width), width)
        return pltpu.make_async_remote_copy(
            src_ref=a_all.at[source * rows : (source + 1) * rows, at],
            dst_ref=a_all.at[target * rows : (target + 1) * rows, at],
            send_sem=send_sem.at[piece],
            recv_sem=recv_sem.at[piece],
            device_id=(rep, device),
            device_id_type=MESH,
        )

    def pair_copy(piece):
        return piece_copy(0, 1, piece, pair_send_sem, pair_recv_sem, partner)

    def y_copy(piece):
        return piece_copy(0, 2, piece, y_send_sem, y_recv_sem, across)

    def pass_copy(piece):
        return piece_copy(2, 3, piece, pass_send_sem, pass_recv_sem, partner)

    @pl.when(step == 0)
    def _():
        barrier = pltpu.get_barrier_semaphore()
        for k in range(1, devices):
            pl.semaphore_signal(barrier, inc=1, device_id=(rep, other(k)), device_id_type=MESH)

    attention_kernel(window_ref, start_ref, weight_ref, query_ref, out_ref, bias_ref)
    a_all[0:rows, pl.ds(pl.multiple_of(step * width, width), width)] = out_ref[...]

    @pl.when(step == 0)
    def _():
        pl.semaphore_wait(pltpu.get_barrier_semaphore(), devices - 1)

    y_copy(step).start()
    pair_copy(step).start()

    @pl.when(step >= LAG)
    def _():
        y_copy(step - LAG).wait_recv()
        pass_copy(step - LAG).start()

    @pl.when(step == steps - 1)
    def _():
        z_low, z_high = lax.rem(z, 2), z // 2
        beside = index_of(z_high * 2 + 1 - z_low, y, core)
        beyond = index_of((1 - z_high) * 2 + z_low, y, core)
        owners = (index_of((1 - z_high) * 2 + 1 - z_low, y, core), beside, beyond, me)

        def strip(owner, first, last):
            at = pl.multiple_of(owner * BLOCK, BLOCK)
            return lax.dot_general(
                a_all[first * rows : last * rows, pl.ds(at, BLOCK)],
                a_all[first * rows : last * rows, pl.ds(at, STRIP)],
                (((0,), (0,)), ((), ())),
                preferred_element_type=jnp.float32,
            )

        def wrap(first, last):
            a_all[first * rows : last * rows, OUT_WIDTH:] = a_all[
                first * rows : last * rows, : STRIP - BLOCK
            ]

        def z_copy(j, half, device):
            at = slice(CUTS[half], CUTS[half + 1])
            return pltpu.make_async_remote_copy(
                src_ref=z_send.at[j, :, at],
                dst_ref=z_recv.at[j, :, at],
                send_sem=z_send_sem.at[j * HALVES + half],
                recv_sem=z_recv_sem.at[j * HALVES + half],
                device_id=(rep, device),
                device_id_type=MESH,
            )

        def forward(piece):
            y_copy(piece).wait_recv()
            pass_copy(piece).start()

        for piece in range(steps):
            pair_copy(piece).wait_recv()
        wrap(0, 2)
        for j in range(4):
            acc[j] = strip(owners[j], 0, 2)
            if j % 2 == 1:
                forward(steps - 2 + j // 2)
        wrap(2, 3)
        acc[0] = acc[0] + strip(owners[0], 2, 3)
        for piece in range(steps):
            pass_copy(piece).wait_recv()
        wrap(3, 4)
        z_send[0] = (acc[0] + strip(owners[0], 3, 4)).astype(jnp.bfloat16)
        for half in range(HALVES):
            z_copy(0, half, beside).start()
        z_send[1] = (acc[1] + strip(owners[1], 2, 4)).astype(jnp.bfloat16)
        for half in range(HALVES):
            z_copy(1, half, beside).start()
        acc[2] = acc[2] + strip(owners[2], 2, 4)
        acc[3] = acc[3] + strip(owners[3], 2, 4)
        for half in range(HALVES):
            at = slice(CUTS[half], CUTS[half + 1])
            z_copy(0, half, beside).wait_recv()
            z_send[2, :, at] = (acc[2, :, at] + z_recv[0, :, at].astype(jnp.float32)).astype(jnp.bfloat16)
            z_copy(2, half, beyond).start()
        t_copies = []
        for half in range(HALVES):
            at = slice(CUTS[half], CUTS[half + 1])
            z_copy(1, half, beside).wait_recv()
            total = acc[3, :, at] + z_recv[1, :, at].astype(jnp.float32)
            z_copy(2, half, beyond).wait_recv()
            acc[3, :, at] = (total + z_recv[2, :, at].astype(jnp.float32)) * inverse_count
            for k in range(max(1, CUTS[half] // BLOCK), min(8, CUTS[half + 1] // BLOCK)):
                t_send[k - 1] = acc[3, :, k * BLOCK : (k + 1) * BLOCK].T.astype(jnp.bfloat16)
                copy = pltpu.make_async_remote_copy(
                    src_ref=t_send.at[k - 1],
                    dst_ref=t_recv.at[k - 1],
                    send_sem=t_send_sem.at[k - 1],
                    recv_sem=t_recv_sem.at[k - 1],
                    device_id=(rep, other(k)),
                    device_id_type=MESH,
                )
                copy.start()
                t_copies.append(copy)
        for k in range(9):
            at = pl.multiple_of(other(k) * BLOCK, BLOCK)
            hessian_ref[:, pl.ds(at, BLOCK)] = acc[3, :, k * BLOCK : (k + 1) * BLOCK]
        for k in range(1, 8):
            t_copies[k - 1].wait_recv()
            at = pl.multiple_of(other(devices - k) * BLOCK, BLOCK)
            hessian_ref[:, pl.ds(at, BLOCK)] = t_recv[k - 1].astype(jnp.float32)
        for piece in range(steps):
            pair_copy(piece).wait_send()
            y_copy(piece).wait_send()
            pass_copy(piece).wait_send()
        for half in range(HALVES):
            z_copy(0, half, beside).wait_send()
            z_copy(1, half, beside).wait_send()
            z_copy(2, half, beyond).wait_send()
        for copy in t_copies:
            copy.wait_send()


def fused(window, start, kv_weight, queries, devices, inverse_count):
    rows = queries.shape[0]
    span = PAIR * PAIRS_PER_STEP
    steps = queries.shape[1] // span

    def body(*refs):
        fused_kernel(devices, inverse_count, *refs)

    return pl.pallas_call(
        body,
        grid=(steps,),
        in_specs=[
            pl.BlockSpec(window.shape, lambda i: (0, 0)),
            pl.BlockSpec(start.shape, lambda i: (0, 0)),
            pl.BlockSpec((KV_RANK, span), lambda i: (0, i)),
            pl.BlockSpec((rows, span), lambda i: (0, i)),
        ],
        out_specs=[
            pl.BlockSpec((rows, PAIRS_PER_STEP * 128), lambda i: (0, i)),
            pl.BlockSpec((BLOCK, OUT_WIDTH), lambda i: (0, 0)),
        ],
        out_shape=[
            jax.ShapeDtypeStruct((rows, OUT_WIDTH), jnp.bfloat16),
            jax.ShapeDtypeStruct((BLOCK, OUT_WIDTH), jnp.float32),
        ],
        scratch_shapes=[
            pltpu.VMEM((rows, 2 * BLOCK), jnp.float32),
            pltpu.VMEM((4 * rows, OUT_WIDTH + STRIP - BLOCK), jnp.bfloat16),
            pltpu.VMEM((4, BLOCK, STRIP), jnp.float32),
            pltpu.VMEM((3, BLOCK, STRIP), jnp.bfloat16),
            pltpu.VMEM((3, BLOCK, STRIP), jnp.bfloat16),
            pltpu.VMEM((7, BLOCK, BLOCK), jnp.bfloat16),
            pltpu.VMEM((7, BLOCK, BLOCK), jnp.bfloat16),
            pltpu.SemaphoreType.DMA((steps,)),
            pltpu.SemaphoreType.DMA((steps,)),
            pltpu.SemaphoreType.DMA((steps,)),
            pltpu.SemaphoreType.DMA((steps,)),
            pltpu.SemaphoreType.DMA((steps,)),
            pltpu.SemaphoreType.DMA((steps,)),
            pltpu.SemaphoreType.DMA((3 * HALVES,)),
            pltpu.SemaphoreType.DMA((3 * HALVES,)),
            pltpu.SemaphoreType.DMA((7,)),
            pltpu.SemaphoreType.DMA((7,)),
        ],
        compiler_params=pltpu.CompilerParams(
            collective_id=0, has_side_effects=True, vmem_limit_bytes=60 * 1024 * 1024
        ),
    )(window, start, kv_weight, queries)


def per_device(queries, latents, kv_weight, lengths):
    devices = lax.axis_size("dp")
    device = lax.axis_index("dp")
    rows = queries.shape[0]
    inverse_count = 1.0 / (rows * devices)
    halo = lax.ppermute(
        latents[rows - MAXLEN :], "dp", [(source, source + 1) for source in range(devices - 1)]
    )
    window = jnp.concatenate([halo, latents], axis=0)
    rope = window[:, KV_RANK:]
    blank = jnp.zeros((rows + MAXLEN, 2 * (128 - ROPE)), window.dtype)
    window = jnp.concatenate([window, blank, rope], axis=1)

    traces = lengths.shape[0]
    order = jnp.arange(traces, dtype=jnp.int32)
    ends = jnp.sum(jnp.where(order[None, :] <= order[:, None], lengths[None, :], 0), axis=1)
    first_row = device * rows
    position = first_row + jnp.arange(rows, dtype=jnp.int32)
    start = jnp.max(jnp.where(ends[None, :] <= position[:, None], ends[None, :], 0), axis=1)
    start = (start - first_row)[:, None]

    if devices == 16:
        attn_out, hessian = fused(window, start, kv_weight, queries, devices, inverse_count)
        return attn_out, hessian
    attn_out = attention(window, start, kv_weight, queries)
    partial = lax.dot_general(
        attn_out, attn_out, (((0,), (0,)), ((), ())), preferred_element_type=jnp.float32
    )
    hessian = lax.psum_scatter(partial, "dp", scatter_dimension=0, tiled=True)
    return attn_out, hessian * inverse_count


def solution(mesh):
    placed = (P(("rep", "dp"), None), P(("rep", "dp"), None), P(), P("rep"))
    return jax.shard_map(
        per_device,
        mesh=mesh,
        in_specs=placed,
        out_specs=(P(("rep", "dp"), None), P(("rep", "dp"), None)),
        check_vma=False,
    )
```
